32 devices in a mesh: row: 8 (over z, x), sub: 4 (over y, core).
Axes of the slice: x: 2, y: 2, z: 4, core: 2. Of those that a mesh axis runs over, the one named last changes fastest.
Arguments:
- eig_vectors: float32 [65536, 512], P(('row', 'sub')), may hold values from -0.0234375 to 0.0234375
- vec_cotangent: float32 [65536, 512], P(('row', 'sub')), may hold values from -768 to 768
- levels: float32 [512], replicated, may hold values from -2 to 2
- order: int32 [512], replicated, may hold values from 0 to 511, each once
- neighbours: int32 [512, 12], P(('row', 'sub')), may hold values from 0 to 511, as said below
Outputs:
- grad_blocks: float32 [512, 12, 128, 128], P(('row', 'sub'))
The draws below stay inside these ranges and needn't reach their ends.
Inputs may be any that keep to these rules, and one draw needn't show every extreme that they name: `neighbours`: entry 0 of row i is i itself. Row blocks are dealt to devices in order, 16 to a device, device index = row index * 4 + sub index; every listed block lies on the row block's own device or on a device whose row index or sub index (not both) differs by one, cyclically.
All inputs are finite; a program needn't handle non-finite values.
Results may differ from the reference program's by a relative error of at most 0.0003.
Values sent between devices are 32-bit elements; how exact they have to be, the bound alone decides.
A program may use at most 192 MiB of HBM per device.

```python
import jax
import jax.numpy as jnp
from jax import lax

WINDOW = 512
BS = 128
NNBR = 12
BLK_DEV = 16
DEV_ROW = 8
DEV_SUB = 4
NBLK = 512
NROWS = 65536


def draw_neighbours(key, part):
    key_dir = jax.random.fold_in(key, 11)
    key_loc = jax.random.fold_in(key, 12)
    blocks = jnp.arange(NBLK, dtype=jnp.int32)
    device = blocks // BLK_DEV
    row_pos = device // DEV_SUB
    sub_pos = device % DEV_SUB
    direction = jax.random.randint(key_dir, (NBLK, NNBR), 0, 5, dtype=jnp.int32)
    local = jax.random.randint(key_loc, (NBLK, NNBR), 0, BLK_DEV, dtype=jnp.int32)
    row_step = jnp.where(direction == 1, 1, jnp.where(direction == 2, -1, 0))
    sub_step = jnp.where(direction == 3, 1, jnp.where(direction == 4, -1, 0))
    row_new = (row_pos[:, None] + row_step + DEV_ROW) % DEV_ROW
    sub_new = (sub_pos[:, None] + sub_step + DEV_SUB) % DEV_SUB
    listed = (row_new * DEV_SUB + sub_new) * BLK_DEV + local
    listed = listed.at[:, 0].set(blocks)
    return listed.astype(jnp.int32)


def level_of(key, dims, shards, low, top_value):
    def one(axis_at, blocks):
        steps = jax.random.uniform(jax.random.fold_in(jax.random.fold_in(key, 6), axis_at), (blocks,), jnp.float32, low / len(shards), top_value / len(shards))
        return jnp.repeat(jnp.exp(steps), dims[axis_at] // blocks).reshape((-1,) + (1,) * (len(dims) - axis_at - 1))

    factor_of = one(*shards[0])
    for cut in shards[1:]:
        factor_of = factor_of * one(*cut)
    return factor_of


def gaussian(key, dims, width, reach, shards=(), kind=jnp.bfloat16):
    gain = level_of(key, dims, shards, -0.22, 0.18) if shards else 1.0
    result = jax.random.normal(key, dims, jnp.float32) * width * gain
    return jnp.minimum(jnp.maximum(result, -reach), reach).astype(kind)


def setup_inputs(seed: int = 0) -> dict:
    keys = jax.random.split(jax.random.key(seed), 6)
    eig_vectors = gaussian(keys[0], (NROWS, WINDOW), NROWS ** -0.5, 0.0234375, ((0, 32),), jnp.float32)
    vec_cotangent = gaussian(keys[1], (NROWS, WINDOW), (NROWS // WINDOW), 768.0, ((0, 32),), jnp.float32)
    levels = jnp.clip(jax.random.uniform(keys[2], (WINDOW,), jnp.float32, -2.0, 2.0), -2.0, 2.0)
    order = jax.random.permutation(keys[3], WINDOW).astype(jnp.int32)
    neighbours = draw_neighbours(jax.random.fold_in(keys[5], 71), 0)
    return dict(eig_vectors=eig_vectors, vec_cotangent=vec_cotangent, levels=levels, order=order, neighbours=neighbours)


broadening_sq = 0.0025


def reference(eig_vectors, vec_cotangent, levels, order, neighbours):
    highest = lax.Precision.HIGHEST
    energy = levels[order.astype(jnp.int32)]
    spread = energy[None, :] - energy[:, None]
    gap_factor = spread / (spread * spread + broadening_sq)
    gram = lax.dot_general(eig_vectors, vec_cotangent, (((0,), (0,)), ((), ())), precision=highest, preferred_element_type=jnp.float32)
    scaled = gap_factor * gram
    adjoint_rows = jnp.dot(eig_vectors, scaled, precision=highest, preferred_element_type=jnp.float32)
    window = eig_vectors.shape[1]
    vec_blocks = eig_vectors.reshape(NBLK, BS, window)
    adj_blocks = adjoint_rows.reshape(NBLK, BS, window)

    def one_block(inputs_pair):
        adj_block, listed = inputs_pair
        picked = vec_blocks[listed.astype(jnp.int32)]
        return jnp.einsum("ak,nbk->nab", adj_block, picked, precision=highest)

    return lax.map(one_block, (adj_blocks, neighbours))
```

```python
import functools

import jax
import jax.numpy as jnp
from jax import lax
from jax.experimental import pallas as pl
from jax.experimental.pallas import tpu as pltpu
from jax.sharding import PartitionSpec as P

BS = 128
PIECE = 256
WIN = 3
LAG = 1

broadening_sq = 0.0025
MESH = pl.DeviceIdType.MESH
F32 = jnp.float32
BF16 = jnp.bfloat16


def split(x):
    hi = x.astype(BF16)
    return hi, (x - hi.astype(F32)).astype(BF16)


def mm(a, b, dims):
    return lax.dot_general(a, b, (dims, ((), ())), preferred_element_type=F32)


def stages_of(n_row, n_sub, window):
    stages = []
    length = window
    for axis, count in (("sub", n_sub), ("row", n_row)):
        mask = 1
        while mask < count:
            halve = length >= 16
            stages.append((axis, mask, length, halve))
            length = length // 2 if halve else length
            mask *= 2
    return stages, length


def halo_kernel(n_row, n_sub, stages, last,
                eig, cot, levels, order, table, wcat,
                qv, vv, acc, full, recv, sh, sl, wv,
                ld_sem, own_sem, w_sem, halo_send, halo_recv, ar_send, ar_recv):
    n_blk = eig.shape[0]
    window = eig.shape[2]
    row = lax.axis_index("row")
    sub = lax.axis_index("sub")
    odd = row % 2
    pair_row = row + 1 - 2 * odd
    ahead = (row + n_row + 2 - 4 * odd) % n_row
    behind = (row + n_row - 2 + 4 * odd) % n_row
    sub_up = (sub + 1) % n_sub
    sub_down = (sub + n_sub - 1) % n_sub

    def flip(axis, mask):
        here = row if axis == "row" else sub
        bit = (here // mask) % 2
        there = here + mask - 2 * mask * bit
        return ((there, sub) if axis == "row" else (row, there)), bit

    partners = [(row, sub_up), (row, sub_down), (pair_row, sub), (ahead, sub), (behind, sub)]
    for axis, mask, _, _ in stages:
        if (axis, mask) not in (("sub", 1), ("row", 1)):
            partners.append(flip(axis, mask)[0])
    barrier = pltpu.get_barrier_semaphore()

    per = PIECE // BS
    n_piece = n_blk // per

    def load(p, which):
        src, dst = ((eig, qv), (cot, vv))[which]
        at = pl.ds(p * per, per)
        return pltpu.make_async_copy(src.at[at], dst.at[at], ld_sem.at[which, p])

    for p in range(n_piece):
        load(p, 0).start()
        load(p, 1).start()
    own = pltpu.make_async_copy(eig, table.at[pl.ds(0, n_blk)], own_sem)
    own.start()

    for there in partners:
        pl.semaphore_signal(barrier, inc=1, device_id=there, device_id_type=MESH)
    pl.semaphore_wait(barrier, len(partners))

    def halo(way, t):
        dev = ((row, sub_up), (row, sub_down), (pair_row, sub), (ahead, sub))[way]
        src = table.at[3 * n_blk + t] if way == 3 else eig.at[t]
        return pltpu.make_async_remote_copy(
            src_ref=src, dst_ref=table.at[(way + 1) * n_blk + t],
            send_sem=halo_send.at[way, t], recv_sem=halo_recv.at[way, t],
            device_id=dev, device_id_type=MESH)

    def gram():
        acc[...] = jnp.zeros_like(acc)

        def body(p, carry):
            load(p, 0).wait()
            load(p, 1).wait()
            at = pl.ds(p * per, per)
            qh, ql = split(qv[at].reshape(PIECE, window))
            vh, vl = split(vv[at].reshape(PIECE, window))
            d = ((0,), (0,))
            acc[...] += mm(qh, vh, d) + (mm(qh, vl, d) + mm(ql, vh, d))
            return carry

        lax.fori_loop(0, n_piece, body, 0)

    offs = [0 * row]
    for axis, mask, length, halve in stages:
        _, bit = flip(axis, mask)
        offs.append(offs[-1] + bit * (length // 2) if halve else offs[-1])
    spans = [s[2] for s in stages] + [last]
    rec_at = [sum(s[2] // 2 if s[3] else s[2] for s in stages[:k]) for k in range(len(stages))]

    def scatter(k):
        axis, mask, length, halve = stages[k]
        dev, bit = flip(axis, mask)
        size = length // 2 if halve else length
        out = offs[k] + (1 - bit) * size if halve else offs[k]
        return pltpu.make_async_remote_copy(
            src_ref=acc.at[pl.ds(pl.multiple_of(out, 8), size)],
            dst_ref=recv.at[pl.ds(rec_at[k], size)],
            send_sem=ar_send.at[0, k], recv_sem=ar_recv.at[0, k],
            device_id=dev, device_id_type=MESH), size

    def scatter_end(k):
        copy, size = scatter(k)
        copy.wait()
        keep = pl.ds(pl.multiple_of(offs[k + 1], 8), size)
        acc[keep] = acc[keep] + recv[pl.ds(rec_at[k], size)]

    def gather(k):
        dev, _ = flip(stages[k][0], stages[k][1])
        at = pl.ds(pl.multiple_of(offs[k + 1], 8), spans[k + 1])
        return pltpu.make_async_remote_copy(
            src_ref=full.at[at], dst_ref=full.at[at],
            send_sem=ar_send.at[1, k], recv_sem=ar_recv.at[1, k],
            device_id=dev, device_id_type=MESH)

    def gather_end(k):
        dev, bit = flip(stages[k][0], stages[k][1])
        copy = gather(k)
        copy.wait_send()
        copy.wait_recv()

    def scale():
        lev = jnp.broadcast_to(levels[...], (window, window)).T
        slot = lax.broadcasted_iota(jnp.int32, (window, window), 0)
        energy = jnp.sum(jnp.where(slot == order[...], lev, 0.0), axis=0, keepdims=True)
        upper = jnp.broadcast_to(energy, (window, window))
        spread = upper - upper.T
        hi, lo = split(spread / (spread * spread + broadening_sq) * full[...])
        sh[...] = hi
        sl[...] = lo

    def adjoint(first, count):
        def body(p, carry):
            qh, ql = split(qv[pl.ds(p * per, per)].reshape(PIECE, window))
            d = ((1,), (0,))
            wh, wl = split(mm(qh, sh[...], d) + (mm(qh, sl[...], d) + mm(ql, sh[...], d)))
            wv[pl.ds(p * per, per), 0] = wh.reshape(per, BS, window)
            wv[pl.ds(p * per, per), 1] = wl.reshape(per, BS, window)
            return carry

        lax.fori_loop(first, first + count, body, 0)

    rounds = [k for k in range(len(stages)) if stages[k][3]]
    jobs = [lambda: None, lambda: None, gram]

    def begin():
        scatter(0)[0].start()

    def middle(k):
        scatter_end(k)
        scatter(k + 1)[0].start()

    def turn():
        scatter_end(len(stages) - 1)
        at = pl.ds(pl.multiple_of(offs[-1], 8), last)
        full[at] = acc[at]
        gather(rounds[-1]).start()

    def back(k, after):
        gather_end(k)
        gather(after).start()

    def finish():
        gather_end(rounds[0])
        scale()

    jobs.append(begin)
    for k in range(len(stages) - 1):
        jobs.append(functools.partial(middle, k))
    jobs.append(turn)
    for k, after in zip(rounds[::-1][:-1], rounds[::-1][1:]):
        jobs.append(functools.partial(back, k, after))
    jobs.append(finish)
    jobs.append(functools.partial(adjoint, 0, n_piece // 2))
    jobs.append(functools.partial(adjoint, n_piece // 2, n_piece - n_piece // 2))

    for t in range(max(n_blk + LAG, len(jobs))):
        if t < n_blk:
            if t >= WIN:
                for way in (0, 1, 2):
                    halo(way, t - WIN).wait_send()
            for way in (2, 0, 1):
                halo(way, t).start()
        if LAG <= t < n_blk + LAG:
            if t >= LAG + WIN:
                halo(3, t - LAG - WIN).wait_send()
            halo(2, t - LAG).wait_recv()
            halo(3, t - LAG).start()
        if t < len(jobs):
            jobs[t]()

    put = pltpu.make_async_copy(wv, wcat, w_sem)
    put.start()
    for t in range(n_blk):
        for way in (0, 1, 3):
            halo(way, t).wait_recv()
    for t in range(n_blk - WIN, n_blk):
        for way in (0, 1, 2, 3):
            halo(way, t).wait_send()
    own.wait()
    put.wait()


def block_kernel(listed, wcat, table, out, buf, sem):
    i = pl.program_id(0)
    n = pl.num_programs(0)
    n_nbr = buf.shape[1]
    window = table.shape[2]

    def fetch(step, k):
        slot = step % 2
        return pltpu.make_async_copy(table.at[listed[step, k]], buf.at[slot, k], sem.at[slot, k])

    @pl.when(i == 0)
    def _():
        for k in range(n_nbr):
            fetch(0, k).start()

    @pl.when(i + 1 < n)
    def _():
        for k in range(n_nbr):
            fetch(i + 1, k).start()

    both = wcat[0].reshape(2 * BS, window)
    d = ((1,), (1,))
    for k in range(0, n_nbr, 2):
        fetch(i, k).wait()
        fetch(i, k + 1).wait()
        qh, ql = split(buf[i % 2, pl.ds(k, 2)].reshape(2 * BS, window))
        big = mm(both, qh, d)
        res = big[:BS] + (big[BS:] + mm(both[:BS], ql, d))
        out[0, k] = res[:, :BS]
        out[0, k + 1] = res[:, BS:]


def body(n_row, n_sub, eig_vectors, vec_cotangent, levels, order, neighbours):
    rows, window = eig_vectors.shape
    n_blk = rows // BS
    n_nbr = neighbours.shape[1]
    eig = eig_vectors.reshape(n_blk, BS, window)
    cot = vec_cotangent.reshape(n_blk, BS, window)
    stages, last = stages_of(n_row, n_sub, window)
    n_rec = sum(s[2] // 2 if s[3] else s[2] for s in stages)
    any_spec = pl.BlockSpec(memory_space=pl.ANY)
    vmem_spec = pl.BlockSpec(memory_space=pltpu.VMEM)
    n_st = len(stages)
    table, wcat = pl.pallas_call(
        functools.partial(halo_kernel, n_row, n_sub, stages, last),
        out_shape=[
            jax.ShapeDtypeStruct((5 * n_blk, BS, window), F32),
            jax.ShapeDtypeStruct((n_blk, 2, BS, window), BF16),
        ],
        in_specs=[any_spec, any_spec, vmem_spec, vmem_spec],
        out_specs=[any_spec, any_spec],
        scratch_shapes=[
            pltpu.VMEM((n_blk, BS, window), F32),
            pltpu.VMEM((n_blk, BS, window), F32),
            pltpu.VMEM((window, window), F32),
            pltpu.VMEM((window, window), F32),
            pltpu.VMEM((n_rec, window), F32),
            pltpu.VMEM((window, window), BF16),
            pltpu.VMEM((window, window), BF16),
            pltpu.VMEM((n_blk, 2, BS, window), BF16),
            pltpu.SemaphoreType.DMA((2, rows // PIECE)),
            pltpu.SemaphoreType.DMA,
            pltpu.SemaphoreType.DMA,
            pltpu.SemaphoreType.DMA((4, n_blk)),
            pltpu.SemaphoreType.DMA((4, n_blk)),
            pltpu.SemaphoreType.DMA((2, n_st)),
            pltpu.SemaphoreType.DMA((2, n_st)),
        ],
        compiler_params=pltpu.CompilerParams(
            collective_id=0, has_side_effects=True, vmem_limit_bytes=48 * 2**20),
        name="halo",
    )(eig, cot, levels.reshape(1, window), order.reshape(1, window))

    my_row = lax.axis_index("row")
    my_sub = lax.axis_index("sub")
    device = neighbours // n_blk
    dev_row = device // n_sub
    dev_sub = device % n_sub
    pair_row = my_row + 1 - 2 * (my_row % 2)
    up = (my_sub + 1) % n_sub
    same_row = jnp.where(dev_sub == my_sub, 0, jnp.where(dev_sub == up, 2, 1))
    slot = jnp.where(dev_row == my_row, same_row, jnp.where(dev_row == pair_row, 3, 4))
    listed = slot * n_blk + neighbours % n_blk

    return pl.pallas_call(
        block_kernel,
        out_shape=jax.ShapeDtypeStruct((n_blk, n_nbr, BS, BS), F32),
        grid_spec=pltpu.PrefetchScalarGridSpec(
            num_scalar_prefetch=1,
            grid=(n_blk,),
            in_specs=[
                pl.BlockSpec((1, 2, BS, window), lambda i, listed: (i, 0, 0, 0)),
                any_spec,
            ],
            out_specs=pl.BlockSpec((1, n_nbr, BS, BS), lambda i, listed: (i, 0, 0, 0)),
            scratch_shapes=[
                pltpu.VMEM((2, n_nbr, BS, window), F32),
                pltpu.SemaphoreType.DMA((2, n_nbr)),
            ],
        ),
        compiler_params=pltpu.CompilerParams(vmem_limit_bytes=48 * 2**20),
        name="blocks",
    )(listed.astype(jnp.int32), wcat, table)


def solution(mesh):
    in_specs = (P(("row", "sub"), None), P(("row", "sub"), None), P(), P(), P(("row", "sub"), None))
    out_specs = P(("row", "sub"), None, None, None)
    run = functools.partial(body, mesh.shape["row"], mesh.shape["sub"])
    return jax.shard_map(run, mesh=mesh, in_specs=in_specs, out_specs=out_specs, check_vma=False)
```

```python
import functools

import jax
import jax.numpy as jnp
from jax import lax
from jax.experimental import pallas as pl
from jax.experimental.pallas import tpu as pltpu
from jax.sharding import PartitionSpec as P

BS = 128
PIECE = 256
CHUNK = 64
WIN = 4
LAG = 1
GAP = 2

broadening_sq = 0.0025
MESH = pl.DeviceIdType.MESH
F32 = jnp.float32
BF16 = jnp.bfloat16


def split(x):
    hi = x.astype(BF16)
    return hi, (x - hi.astype(F32)).astype(BF16)


def mm(a, b, dims):
    return lax.dot_general(a, b, (dims, ((), ())), preferred_element_type=F32)


def stages_of(n_row, n_sub, window):
    stages = []
    length = window
    for axis, count in (("sub", n_sub), ("row", n_row)):
        mask = 1
        while mask < count:
            halve = length >= 16
            stages.append((axis, mask, length, halve))
            length = length // 2 if halve else length
            mask *= 2
    return stages, length


def halo_kernel(n_row, n_sub, stages, last,
                eig, cot, levels, order, table, wcat,
                qv, vv, acc, full, recv, sh, sl, wv,
                ld_sem, own_sem, w_sem, halo_send, halo_recv, ar_send, ar_recv):
    n_chunk = eig.shape[0]
    window = eig.shape[2]
    row = lax.axis_index("row")
    sub = lax.axis_index("sub")
    odd = row % 2
    pair_row = row + 1 - 2 * odd
    ahead = (row + n_row + 2 - 4 * odd) % n_row
    behind = (row + n_row - 2 + 4 * odd) % n_row
    sub_up = (sub + 1) % n_sub
    sub_down = (sub + n_sub - 1) % n_sub

    def flip(axis, mask):
        here = row if axis == "row" else sub
        bit = (here // mask) % 2
        there = here + mask - 2 * mask * bit
        return ((there, sub) if axis == "row" else (row, there)), bit

    partners = [(row, sub_up), (row, sub_down), (pair_row, sub), (ahead, sub), (behind, sub)]
    for axis, mask, _, _ in stages:
        if (axis, mask) not in (("sub", 1), ("row", 1)):
            partners.append(flip(axis, mask)[0])
    barrier = pltpu.get_barrier_semaphore()

    per = PIECE // CHUNK
    blocks = PIECE // BS
    n_piece = n_chunk // per

    def load(p, which):
        src, dst = ((eig, qv), (cot, vv))[which]
        at = pl.ds(p * per, per)
        return pltpu.make_async_copy(src.at[at], dst.at[at], ld_sem.at[which, p])

    for p in range(n_piece):
        load(p, 0).start()
        load(p, 1).start()
    own = pltpu.make_async_copy(eig, table.at[pl.ds(0, n_chunk)], own_sem)
    own.start()

    for there in partners:
        pl.semaphore_signal(barrier, inc=1, device_id=there, device_id_type=MESH)
    pl.semaphore_wait(barrier, len(partners))

    def halo(way, t):
        dev = ((row, sub_up), (row, sub_down), (pair_row, sub), (ahead, sub))[way]
        src = table.at[3 * n_chunk + t] if way == 3 else eig.at[t]
        return pltpu.make_async_remote_copy(
            src_ref=src, dst_ref=table.at[(way + 1) * n_chunk + t],
            send_sem=halo_send.at[way, t], recv_sem=halo_recv.at[way, t],
            device_id=dev, device_id_type=MESH)

    def gram():
        acc[...] = jnp.zeros_like(acc)

        def body(p, carry):
            load(p, 0).wait()
            load(p, 1).wait()
            at = pl.ds(p * per, per)
            qh, ql = split(qv[at].reshape(PIECE, window))
            vh, vl = split(vv[at].reshape(PIECE, window))
            d = ((0,), (0,))
            acc[...] += mm(qh, vh, d) + (mm(qh, vl, d) + mm(ql, vh, d))
            return carry

        lax.fori_loop(0, n_piece, body, 0)

    offs = [0 * row]
    for axis, mask, length, halve in stages:
        _, bit = flip(axis, mask)
        offs.append(offs[-1] + bit * (length // 2) if halve else offs[-1])
    spans = [s[2] for s in stages] + [last]
    rec_at = [sum(s[2] // 2 if s[3] else s[2] for s in stages[:k]) for k in range(len(stages))]

    def scatter(k):
        axis, mask, length, halve = stages[k]
        dev, bit = flip(axis, mask)
        size = length // 2 if halve else length
        out = offs[k] + (1 - bit) * size if halve else offs[k]
        return pltpu.make_async_remote_copy(
            src_ref=acc.at[pl.ds(pl.multiple_of(out, 8), size)],
            dst_ref=recv.at[pl.ds(rec_at[k], size)],
            send_sem=ar_send.at[0, k], recv_sem=ar_recv.at[0, k],
            device_id=dev, device_id_type=MESH), size

    def scatter_end(k):
        copy, size = scatter(k)
        copy.wait()
        keep = pl.ds(pl.multiple_of(offs[k + 1], 8), size)
        acc[keep] = acc[keep] + recv[pl.ds(rec_at[k], size)]

    def gather(k):
        dev, _ = flip(stages[k][0], stages[k][1])
        at = pl.ds(pl.multiple_of(offs[k + 1], 8), spans[k + 1])
        return pltpu.make_async_remote_copy(
            src_ref=full.at[at], dst_ref=full.at[at],
            send_sem=ar_send.at[1, k], recv_sem=ar_recv.at[1, k],
            device_id=dev, device_id_type=MESH)

    def gather_end(k):
        dev, bit = flip(stages[k][0], stages[k][1])
        copy = gather(k)
        copy.wait_send()
        copy.wait_recv()

    def scale():
        lev = jnp.broadcast_to(levels[...], (window, window)).T
        slot = lax.broadcasted_iota(jnp.int32, (window, window), 0)
        energy = jnp.sum(jnp.where(slot == order[...], lev, 0.0), axis=0, keepdims=True)
        upper = jnp.broadcast_to(energy, (window, window))
        spread = upper - upper.T
        hi, lo = split(spread / (spread * spread + broadening_sq) * full[...])
        sh[...] = hi
        sl[...] = lo

    def adjoint(first, count):
        def body(p, carry):
            qh, ql = split(qv[pl.ds(p * per, per)].reshape(PIECE, window))
            d = ((1,), (0,))
            w = mm(qh, sh[...], d) + (mm(qh, sl[...], d) + mm(ql, sh[...], d))
            for b in range(blocks):
                hi, lo = split(w[b * BS:(b + 1) * BS].T)
                wv[p * blocks + b, :, :BS] = hi
                wv[p * blocks + b, :, BS:] = lo
            return carry

        lax.fori_loop(first, first + count, body, 0)

    rounds = [k for k in range(len(stages)) if stages[k][3]]
    def begin():
        scatter(0)[0].start()

    def middle(k):
        scatter_end(k)
        scatter(k + 1)[0].start()

    def turn():
        scatter_end(len(stages) - 1)
        at = pl.ds(pl.multiple_of(offs[-1], 8), last)
        full[at] = acc[at]
        gather(rounds[-1]).start()

    def back(k, after):
        gather_end(k)
        gather(after).start()

    def finish():
        gather_end(rounds[0])
        scale()

    jobs = {WIN - 1: gram, WIN: begin}
    at_step = WIN + GAP
    for k in range(len(stages) - 1):
        jobs[at_step] = functools.partial(middle, k)
        at_step += GAP
    jobs[at_step] = turn
    at_step += GAP
    for k, after in zip(rounds[::-1][:-1], rounds[::-1][1:]):
        jobs[at_step] = functools.partial(back, k, after)
        at_step += GAP
    jobs[at_step] = finish
    for p in range(0, n_piece, 2):
        at_step += 1
        jobs[at_step] = functools.partial(adjoint, p, 2)

    for t in range(max(n_chunk + LAG, max(jobs) + 1)):
        if t < n_chunk:
            if t >= WIN:
                for way in (0, 1, 2):
                    halo(way, t - WIN).wait_send()
            for way in (2, 0, 1):
                halo(way, t).start()
        if LAG <= t < n_chunk + LAG:
            if t >= LAG + WIN:
                halo(3, t - LAG - WIN).wait_send()
            halo(2, t - LAG).wait_recv()
            halo(3, t - LAG).start()
        if t in jobs:
            jobs[t]()

    put = pltpu.make_async_copy(wv, wcat, w_sem)
    put.start()
    for t in range(n_chunk):
        for way in (0, 1, 3):
            halo(way, t).wait_recv()
    for t in range(n_chunk - WIN, n_chunk):
        for way in (0, 1, 2, 3):
            halo(way, t).wait_send()
    own.wait()
    put.wait()


def block_kernel(listed, wcat, table, out, buf, sem):
    i = pl.program_id(0)
    n = pl.num_programs(0)
    n_nbr = buf.shape[1]
    window = table.shape[2]

    def fetch(step, k):
        slot = step % 2
        return pltpu.make_async_copy(table.at[listed[step, k]], buf.at[slot, k], sem.at[slot, k])

    @pl.when(i == 0)
    def _():
        for k in range(n_nbr):
            fetch(0, k).start()

    @pl.when(i + 1 < n)
    def _():
        for k in range(n_nbr):
            fetch(i + 1, k).start()

    d = ((1,), (0,))
    group = n_nbr // 2
    for first in range(0, n_nbr, group):
        for k in range(first, first + group):
            fetch(i, k).wait()
        qh, ql = split(buf[i % 2, pl.ds(first, group)].reshape(group * BS, window))
        big = mm(qh, wcat[0], d)
        res = big[:, :BS] + (big[:, BS:] + mm(ql, wcat[0, :, :BS], d))
        for k in range(group):
            out[0, first + k] = res[k * BS:(k + 1) * BS].T


def body(n_row, n_sub, eig_vectors, vec_cotangent, levels, order, neighbours):
    rows, window = eig_vectors.shape
    n_blk = rows // BS
    n_nbr = neighbours.shape[1]
    n_chunk = rows // CHUNK
    eig = eig_vectors.reshape(n_chunk, CHUNK, window)
    cot = vec_cotangent.reshape(n_chunk, CHUNK, window)
    stages, last = stages_of(n_row, n_sub, window)
    n_rec = sum(s[2] // 2 if s[3] else s[2] for s in stages)
    any_spec = pl.BlockSpec(memory_space=pl.ANY)
    vmem_spec = pl.BlockSpec(memory_space=pltpu.VMEM)
    n_st = len(stages)
    table, wcat = pl.pallas_call(
        functools.partial(halo_kernel, n_row, n_sub, stages, last),
        out_shape=[
            jax.ShapeDtypeStruct((5 * n_chunk, CHUNK, window), F32),
            jax.ShapeDtypeStruct((n_blk, window, 2 * BS), BF16),
        ],
        in_specs=[any_spec, any_spec, vmem_spec, vmem_spec],
        out_specs=[any_spec, any_spec],
        scratch_shapes=[
            pltpu.VMEM((n_chunk, CHUNK, window), F32),
            pltpu.VMEM((n_chunk, CHUNK, window), F32),
            pltpu.VMEM((window, window), F32),
            pltpu.VMEM((window, window), F32),
            pltpu.VMEM((n_rec, window), F32),
            pltpu.VMEM((window, window), BF16),
            pltpu.VMEM((window, window), BF16),
            pltpu.VMEM((n_blk, window, 2 * BS), BF16),
            pltpu.SemaphoreType.DMA((2, rows // PIECE)),
            pltpu.SemaphoreType.DMA,
            pltpu.SemaphoreType.DMA,
            pltpu.SemaphoreType.DMA((4, n_chunk)),
            pltpu.SemaphoreType.DMA((4, n_chunk)),
            pltpu.SemaphoreType.DMA((2, n_st)),
            pltpu.SemaphoreType.DMA((2, n_st)),
        ],
        compiler_params=pltpu.CompilerParams(
            collective_id=0, has_side_effects=True, vmem_limit_bytes=48 * 2**20),
        name="halo",
    )(eig, cot, levels.reshape(1, window), order.reshape(1, window))

    my_row = lax.axis_index("row")
    my_sub = lax.axis_index("sub")
    device = neighbours // n_blk
    dev_row = device // n_sub
    dev_sub = device % n_sub
    pair_row = my_row + 1 - 2 * (my_row % 2)
    up = (my_sub + 1) % n_sub
    same_row = jnp.where(dev_sub == my_sub, 0, jnp.where(dev_sub == up, 2, 1))
    slot = jnp.where(dev_row == my_row, same_row, jnp.where(dev_row == pair_row, 3, 4))
    listed = slot * n_blk + neighbours % n_blk

    return pl.pallas_call(
        block_kernel,
        out_shape=jax.ShapeDtypeStruct((n_blk, n_nbr, BS, BS), F32),
        grid_spec=pltpu.PrefetchScalarGridSpec(
            num_scalar_prefetch=1,
            grid=(n_blk,),
            in_specs=[
                pl.BlockSpec((1, window, 2 * BS), lambda i, listed: (i, 0, 0)),
                any_spec,
            ],
            out_specs=pl.BlockSpec((1, n_nbr, BS, BS), lambda i, listed: (i, 0, 0, 0)),
            scratch_shapes=[
                pltpu.VMEM((2, n_nbr, BS, window), F32),
                pltpu.SemaphoreType.DMA((2, n_nbr)),
            ],
        ),
        compiler_params=pltpu.CompilerParams(vmem_limit_bytes=48 * 2**20),
        name="blocks",
    )(listed.astype(jnp.int32), wcat, table.reshape(5 * n_blk, BS, window))


def solution(mesh):
    in_specs = (P(("row", "sub"), None), P(("row", "sub"), None), P(), P(), P(("row", "sub"), None))
    out_specs = P(("row", "sub"), None, None, None)
    run = functools.partial(body, mesh.shape["row"], mesh.shape["sub"])
    return jax.shard_map(run, mesh=mesh, in_specs=in_specs, out_specs=out_specs, check_vma=False)
```

```python
import functools

import jax
import jax.numpy as jnp
from jax import lax
from jax.experimental import pallas as pl
from jax.experimental.pallas import tpu as pltpu
from jax.sharding import PartitionSpec as P

BS = 128
PIECE = 256
CHUNK = 64
WIN = 6
LAG = 4
GAP = 2

broadening_sq = 0.0025
MESH = pl.DeviceIdType.MESH
F32 = jnp.float32
BF16 = jnp.bfloat16


def split(x):
    hi = x.astype(BF16)
    return hi, (x - hi.astype(F32)).astype(BF16)


def mm(a, b, dims):
    return lax.dot_general(a, b, (dims, ((), ())), preferred_element_type=F32)


def stages_of(n_row, n_sub, window):
    stages = []
    length = window
    for axis, count in (("sub", n_sub), ("row", n_row)):
        mask = 1
        while mask < count:
            halve = length >= 16
            stages.append((axis, mask, length, halve))
            length = length // 2 if halve else length
            mask *= 2
    return stages, length


def halo_kernel(n_row, n_sub, stages, last,
                eig, cot, levels, order, table, wcat,
                qv, vv, acc, full, recv, sh, sl, wv,
                ld_sem, own_sem, w_sem, halo_send, halo_recv, ar_send, ar_recv):
    n_chunk = eig.shape[0]
    window = eig.shape[2]
    row = lax.axis_index("row")
    sub = lax.axis_index("sub")
    odd = row % 2
    pair_row = row + 1 - 2 * odd
    ahead = (row + n_row + 2 - 4 * odd) % n_row
    behind = (row + n_row - 2 + 4 * odd) % n_row
    sub_up = (sub + 1) % n_sub
    sub_down = (sub + n_sub - 1) % n_sub

    def flip(axis, mask):
        here = row if axis == "row" else sub
        bit = (here // mask) % 2
        there = here + mask - 2 * mask * bit
        return ((there, sub) if axis == "row" else (row, there)), bit

    partners = [(row, sub_up), (row, sub_down), (pair_row, sub), (ahead, sub), (behind, sub)]
    for axis, mask, _, _ in stages:
        if (axis, mask) not in (("sub", 1), ("row", 1)):
            partners.append(flip(axis, mask)[0])
    barrier = pltpu.get_barrier_semaphore()

    per = PIECE // CHUNK
    blocks = PIECE // BS
    n_piece = n_chunk // per

    def load(p, which):
        src, dst = ((eig, qv), (cot, vv))[which]
        at = pl.ds(p * per, per)
        return pltpu.make_async_copy(src.at[at], dst.at[at], ld_sem.at[which, p])

    for p in range(n_piece):
        load(p, 0).start()
        load(p, 1).start()
    own = pltpu.make_async_copy(eig, table.at[pl.ds(0, n_chunk)], own_sem)
    own.start()

    acc[...] = jnp.zeros_like(acc)
    for there in partners:
        pl.semaphore_signal(barrier, inc=1, device_id=there, device_id_type=MESH)
    pl.semaphore_wait(barrier, len(partners))

    def halo(way, t):
        dev = ((row, sub_up), (row, sub_down), (pair_row, sub), (ahead, sub))[way]
        src = table.at[3 * n_chunk + t] if way == 3 else eig.at[t]
        return pltpu.make_async_remote_copy(
            src_ref=src, dst_ref=table.at[(way + 1) * n_chunk + t],
            send_sem=halo_send.at[way, t], recv_sem=halo_recv.at[way, t],
            device_id=dev, device_id_type=MESH)

    def gram(first, count):
        def body(p, carry):
            load(p, 0).wait()
            load(p, 1).wait()
            at = pl.ds(p * per, per)
            qh, ql = split(qv[at].reshape(PIECE, window))
            vh, vl = split(vv[at].reshape(PIECE, window))
            d = ((0,), (0,))
            acc[...] += mm(qh, vh, d) + (mm(qh, vl, d) + mm(ql, vh, d))
            return carry

        lax.fori_loop(first, first + count, body, 0)

    offs = [0 * row]
    for axis, mask, length, halve in stages:
        _, bit = flip(axis, mask)
        offs.append(offs[-1] + bit * (length // 2) if halve else offs[-1])
    spans = [s[2] for s in stages] + [last]
    rec_at = [sum(s[2] // 2 if s[3] else s[2] for s in stages[:k]) for k in range(len(stages))]

    def scatter(k):
        axis, mask, length, halve = stages[k]
        dev, bit = flip(axis, mask)
        size = length // 2 if halve else length
        out = offs[k] + (1 - bit) * size if halve else offs[k]
        return pltpu.make_async_remote_copy(
            src_ref=acc.at[pl.ds(pl.multiple_of(out, 8), size)],
            dst_ref=recv.at[pl.ds(rec_at[k], size)],
            send_sem=ar_send.at[0, k], recv_sem=ar_recv.at[0, k],
            device_id=dev, device_id_type=MESH), size

    def scatter_end(k):
        copy, size = scatter(k)
        copy.wait()
        keep = pl.ds(pl.multiple_of(offs[k + 1], 8), size)
        acc[keep] = acc[keep] + recv[pl.ds(rec_at[k], size)]

    def gather(k):
        dev, _ = flip(stages[k][0], stages[k][1])
        at = pl.ds(pl.multiple_of(offs[k + 1], 8), spans[k + 1])
        return pltpu.make_async_remote_copy(
            src_ref=full.at[at], dst_ref=full.at[at],
            send_sem=ar_send.at[1, k], recv_sem=ar_recv.at[1, k],
            device_id=dev, device_id_type=MESH)

    def gather_end(k):
        dev, bit = flip(stages[k][0], stages[k][1])
        copy = gather(k)
        copy.wait_send()
        copy.wait_recv()

    def scale():
        lev = jnp.broadcast_to(levels[...], (window, window)).T
        slot = lax.broadcasted_iota(jnp.int32, (window, window), 0)
        energy = jnp.sum(jnp.where(slot == order[...], lev, 0.0), axis=0, keepdims=True)
        upper = jnp.broadcast_to(energy, (window, window))
        spread = upper - upper.T
        hi, lo = split(spread / (spread * spread + broadening_sq) * full[...])
        sh[...] = hi
        sl[...] = lo

    def adjoint(first, count):
        def body(p, carry):
            qh, ql = split(qv[pl.ds(p * per, per)].reshape(PIECE, window))
            d = ((1,), (0,))
            w = mm(qh, sh[...], d) + (mm(qh, sl[...], d) + mm(ql, sh[...], d))
            for b in range(blocks):
                hi, lo = split(w[b * BS:(b + 1) * BS].T)
                wv[p * blocks + b, :, :BS] = hi
                wv[p * blocks + b, :, BS:] = lo
            return carry

        lax.fori_loop(first, first + count, body, 0)

    rounds = [k for k in range(len(stages)) if stages[k][3]]
    def begin():
        scatter(0)[0].start()

    def middle(k):
        scatter_end(k)
        scatter(k + 1)[0].start()

    def turn():
        scatter_end(len(stages) - 1)
        at = pl.ds(pl.multiple_of(offs[-1], 8), last)
        full[at] = acc[at]
        gather(rounds[-1]).start()

    def back(k, after):
        gather_end(k)
        gather(after).start()

    def finish():
        gather_end(rounds[0])
        scale()

    jobs = {}
    at_step = LAG
    for p in range(0, n_piece, 2):
        jobs[at_step] = functools.partial(gram, p, 2)
        at_step += 1
    jobs[at_step] = begin
    at_step += GAP
    for k in range(len(stages) - 1):
        jobs[at_step] = functools.partial(middle, k)
        at_step += GAP
    jobs[at_step] = turn
    at_step += GAP
    for k, after in zip(rounds[::-1][:-1], rounds[::-1][1:]):
        jobs[at_step] = functools.partial(back, k, after)
        at_step += GAP
    jobs[at_step] = finish
    for p in range(0, n_piece, 2):
        at_step += 1
        jobs[at_step] = functools.partial(adjoint, p, 2)

    for t in range(max(n_chunk + LAG, max(jobs) + 1)):
        if t < n_chunk:
            if t >= WIN:
                for way in (0, 1, 2):
                    halo(way, t - WIN).wait_send()
            for way in (2, 0, 1):
                halo(way, t).start()
        if LAG <= t < n_chunk + LAG:
            if t >= LAG + WIN:
                halo(3, t - LAG - WIN).wait_send()
            halo(2, t - LAG).wait_recv()
            halo(3, t - LAG).start()
        if t in jobs:
            jobs[t]()

    put = pltpu.make_async_copy(wv, wcat, w_sem)
    put.start()
    for t in range(n_chunk):
        for way in (0, 1, 3):
            halo(way, t).wait_recv()
    for t in range(n_chunk - WIN, n_chunk):
        for way in (0, 1, 2, 3):
            halo(way, t).wait_send()
    own.wait()
    put.wait()


def block_kernel(listed, wcat, table, out, buf, sem):
    i = pl.program_id(0)
    n = pl.num_programs(0)
    n_nbr = buf.shape[1]
    window = table.shape[2]

    def fetch(step, k):
        slot = step % 2
        return pltpu.make_async_copy(table.at[listed[step, k]], buf.at[slot, k], sem.at[slot, k])

    @pl.when(i == 0)
    def _():
        for k in range(n_nbr):
            fetch(0, k).start()

    @pl.when(i + 1 < n)
    def _():
        for k in range(n_nbr):
            fetch(i + 1, k).start()

    d = ((1,), (0,))
    for k in range(n_nbr):
        fetch(i, k).wait()
    group = 4
    for first in range(0, n_nbr, group):
        qh, ql = split(buf[i % 2, pl.ds(first, group)].reshape(group * BS, window))
        big = mm(qh, wcat[0], d)
        res = big[:, :BS] + (big[:, BS:] + mm(ql, wcat[0, :, :BS], d))
        for k in range(group):
            out[0, first + k] = res[k * BS:(k + 1) * BS].T


def body(n_row, n_sub, eig_vectors, vec_cotangent, levels, order, neighbours):
    rows, window = eig_vectors.shape
    n_blk = rows // BS
    n_nbr = neighbours.shape[1]
    n_chunk = rows // CHUNK
    eig = eig_vectors.reshape(n_chunk, CHUNK, window)
    cot = vec_cotangent.reshape(n_chunk, CHUNK, window)
    stages, last = stages_of(n_row, n_sub, window)
    n_rec = sum(s[2] // 2 if s[3] else s[2] for s in stages)
    any_spec = pl.BlockSpec(memory_space=pl.ANY)
    vmem_spec = pl.BlockSpec(memory_space=pltpu.VMEM)
    n_st = len(stages)
    table, wcat = pl.pallas_call(
        functools.partial(halo_kernel, n_row, n_sub, stages, last),
        out_shape=[
            jax.ShapeDtypeStruct((5 * n_chunk, CHUNK, window), F32),
            jax.ShapeDtypeStruct((n_blk, window, 2 * BS), BF16),
        ],
        in_specs=[any_spec, any_spec, vmem_spec, vmem_spec],
        out_specs=[any_spec, any_spec],
        scratch_shapes=[
            pltpu.VMEM((n_chunk, CHUNK, window), F32),
            pltpu.VMEM((n_chunk, CHUNK, window), F32),
            pltpu.VMEM((window, window), F32),
            pltpu.VMEM((window, window), F32),
            pltpu.VMEM((n_rec, window), F32),
            pltpu.VMEM((window, window), BF16),
            pltpu.VMEM((window, window), BF16),
            pltpu.VMEM((n_blk, window, 2 * BS), BF16),
            pltpu.SemaphoreType.DMA((2, rows // PIECE)),
            pltpu.SemaphoreType.DMA,
            pltpu.SemaphoreType.DMA,
            pltpu.SemaphoreType.DMA((4, n_chunk)),
            pltpu.SemaphoreType.DMA((4, n_chunk)),
            pltpu.SemaphoreType.DMA((2, n_st)),
            pltpu.SemaphoreType.DMA((2, n_st)),
        ],
        compiler_params=pltpu.CompilerParams(
            collective_id=0, has_side_effects=True, vmem_limit_bytes=48 * 2**20),
        name="halo",
    )(eig, cot, levels.reshape(1, window), order.reshape(1, window))

    my_row = lax.axis_index("row")
    my_sub = lax.axis_index("sub")
    device = neighbours // n_blk
    dev_row = device // n_sub
    dev_sub = device % n_sub
    pair_row = my_row + 1 - 2 * (my_row % 2)
    up = (my_sub + 1) % n_sub
    same_row = jnp.where(dev_sub == my_sub, 0, jnp.where(dev_sub == up, 2, 1))
    slot = jnp.where(dev_row == my_row, same_row, jnp.where(dev_row == pair_row, 3, 4))
    listed = slot * n_blk + neighbours % n_blk

    return pl.pallas_call(
        block_kernel,
        out_shape=jax.ShapeDtypeStruct((n_blk, n_nbr, BS, BS), F32),
        grid_spec=pltpu.PrefetchScalarGridSpec(
            num_scalar_prefetch=1,
            grid=(n_blk,),
            in_specs=[
                pl.BlockSpec((1, window, 2 * BS), lambda i, listed: (i, 0, 0)),
                any_spec,
            ],
            out_specs=pl.BlockSpec((1, n_nbr, BS, BS), lambda i, listed: (i, 0, 0, 0)),
            scratch_shapes=[
                pltpu.VMEM((2, n_nbr, BS, window), F32),
                pltpu.SemaphoreType.DMA((2, n_nbr)),
            ],
        ),
        compiler_params=pltpu.CompilerParams(vmem_limit_bytes=48 * 2**20),
        name="blocks",
    )(listed.astype(jnp.int32), wcat, table.reshape(5 * n_blk, BS, window))


def solution(mesh):
    in_specs = (P(("row", "sub"), None), P(("row", "sub"), None), P(), P(), P(("row", "sub"), None))
    out_specs = P(("row", "sub"), None, None, None)
    run = functools.partial(body, mesh.shape["row"], mesh.shape["sub"])
    return jax.shard_map(run, mesh=mesh, in_specs=in_specs, out_specs=out_specs, check_vma=False)
```

```python
import functools

import jax
import jax.numpy as jnp
from jax import lax
from jax.experimental import pallas as pl
from jax.experimental.pallas import tpu as pltpu
from jax.sharding import PartitionSpec as P

BS = 128
PIECE = 256
CHUNK = 64
WIN = 6
LAG = 4
GAP = 1

broadening_sq = 0.0025
MESH = pl.DeviceIdType.MESH
F32 = jnp.float32
BF16 = jnp.bfloat16


def split(x):
    hi = x.astype(BF16)
    return hi, (x - hi.astype(F32)).astype(BF16)


def mm(a, b, dims):
    return lax.dot_general(a, b, (dims, ((), ())), preferred_element_type=F32)


def stages_of(n_row, n_sub, window):
    stages = []
    length = window
    for axis, count in (("sub", n_sub), ("row", n_row)):
        mask = 1
        while mask < count:
            halve = length >= 16
            stages.append((axis, mask, length, halve))
            length = length // 2 if halve else length
            mask *= 2
    return stages, length


def halo_kernel(n_row, n_sub, stages, last,
                eig, cot, levels, order, picks, table, wcat, early,
                near, vv, ev, acc, full, recv, sh, sl, wv,
                ld_sem, e_sem, w_sem, halo_send, halo_recv, ar_send, ar_recv):
    n_chunk = eig.shape[0]
    window = eig.shape[2]
    row = lax.axis_index("row")
    sub = lax.axis_index("sub")
    odd = row % 2
    pair_row = row + 1 - 2 * odd
    ahead = (row + n_row + 2 - 4 * odd) % n_row
    behind = (row + n_row - 2 + 4 * odd) % n_row
    sub_up = (sub + 1) % n_sub
    sub_down = (sub + n_sub - 1) % n_sub

    def flip(axis, mask):
        here = row if axis == "row" else sub
        bit = (here // mask) % 2
        there = here + mask - 2 * mask * bit
        return ((there, sub) if axis == "row" else (row, there)), bit

    partners = [(row, sub_up), (row, sub_down), (pair_row, sub), (ahead, sub), (behind, sub)]
    for axis, mask, _, _ in stages:
        if (axis, mask) not in (("sub", 1), ("row", 1)):
            partners.append(flip(axis, mask)[0])
    barrier = pltpu.get_barrier_semaphore()

    per = PIECE // CHUNK
    blocks = PIECE // BS
    n_piece = n_chunk // per
    n_near = (near.shape[0] - n_chunk) // 4
    n_far = n_chunk - n_near
    n_blk = n_chunk * CHUNK // BS
    two = BS // CHUNK

    def load(p, which):
        src, dst = ((eig, near), (cot, vv))[which]
        at = pl.ds(p * per, per)
        return pltpu.make_async_copy(src.at[at], dst.at[at], ld_sem.at[which, p])

    for p in range(n_piece):
        load(p, 0).start()
        load(p, 1).start()

    acc[...] = jnp.zeros_like(acc)
    for there in partners:
        pl.semaphore_signal(barrier, inc=1, device_id=there, device_id_type=MESH)
    pl.semaphore_wait(barrier, len(partners))

    def halo(way, t):
        dev = ((row, sub_up), (row, sub_down), (pair_row, sub), (ahead, sub))[way]
        def place(way):
            if t < n_near:
                return near.at[n_chunk + way * n_near + t]
            return table.at[way * n_far + t - n_near]

        src = place(2) if way == 3 else eig.at[t]
        return pltpu.make_async_remote_copy(
            src_ref=src, dst_ref=place(way),
            send_sem=halo_send.at[way, t], recv_sem=halo_recv.at[way, t],
            device_id=dev, device_id_type=MESH)

    def gram(first, count):
        def body(p, carry):
            load(p, 0).wait()
            load(p, 1).wait()
            at = pl.ds(p * per, per)
            qh, ql = split(near[at].reshape(PIECE, window))
            vh, vl = split(vv[at].reshape(PIECE, window))
            d = ((0,), (0,))
            acc[...] += mm(qh, vh, d) + (mm(qh, vl, d) + mm(ql, vh, d))
            return carry

        lax.fori_loop(first, first + count, body, 0)

    offs = [0 * row]
    for axis, mask, length, halve in stages:
        _, bit = flip(axis, mask)
        offs.append(offs[-1] + bit * (length // 2) if halve else offs[-1])
    spans = [s[2] for s in stages] + [last]
    rec_at = [sum(s[2] // 2 if s[3] else s[2] for s in stages[:k]) for k in range(len(stages))]

    def scatter(k):
        axis, mask, length, halve = stages[k]
        dev, bit = flip(axis, mask)
        size = length // 2 if halve else length
        out = offs[k] + (1 - bit) * size if halve else offs[k]
        return pltpu.make_async_remote_copy(
            src_ref=acc.at[pl.ds(pl.multiple_of(out, 8), size)],
            dst_ref=recv.at[pl.ds(rec_at[k], size)],
            send_sem=ar_send.at[0, k], recv_sem=ar_recv.at[0, k],
            device_id=dev, device_id_type=MESH), size

    def scatter_end(k):
        copy, size = scatter(k)
        copy.wait()
        keep = pl.ds(pl.multiple_of(offs[k + 1], 8), size)
        acc[keep] = acc[keep] + recv[pl.ds(rec_at[k], size)]

    def gather(k):
        dev, _ = flip(stages[k][0], stages[k][1])
        at = pl.ds(pl.multiple_of(offs[k + 1], 8), spans[k + 1])
        return pltpu.make_async_remote_copy(
            src_ref=full.at[at], dst_ref=full.at[at],
            send_sem=ar_send.at[1, k], recv_sem=ar_recv.at[1, k],
            device_id=dev, device_id_type=MESH)

    def gather_end(k):
        dev, bit = flip(stages[k][0], stages[k][1])
        copy = gather(k)
        copy.wait_send()
        copy.wait_recv()

    def scale():
        lev = jnp.broadcast_to(levels[...], (window, window)).T
        slot = lax.broadcasted_iota(jnp.int32, (window, window), 0)
        energy = jnp.sum(jnp.where(slot == order[...], lev, 0.0), axis=0, keepdims=True)
        upper = jnp.broadcast_to(energy, (window, window))
        spread = upper - upper.T
        hi, lo = split(spread / (spread * spread + broadening_sq) * full[...])
        sh[...] = hi
        sl[...] = lo

    def adjoint(first, count):
        def body(p, carry):
            qh, ql = split(near[pl.ds(p * per, per)].reshape(PIECE, window))
            d = ((1,), (0,))
            w = mm(qh, sh[...], d) + (mm(qh, sl[...], d) + mm(ql, sh[...], d))
            for b in range(blocks):
                hi, lo = split(w[b * BS:(b + 1) * BS].T)
                wv[p * blocks + b, :, :BS] = hi
                wv[p * blocks + b, :, BS:] = lo
            return carry

        lax.fori_loop(first, first + count, body, 0)

    def put_early(i):
        return pltpu.make_async_copy(ev.at[i % 2], early.at[i], e_sem.at[i % 2])

    def products(first, count):
        n_nbr = ev.shape[1]
        group = n_nbr // 2

        def body(i, carry):
            @pl.when(i >= 2)
            def _():
                put_early(i - 2).wait()

            for g in range(0, n_nbr, group):
                rows = [near[pl.ds(picks[i, g + k] * two, two)].reshape(BS, window) for k in range(group)]
                qh, ql = split(jnp.concatenate(rows, axis=0))
                d = ((1,), (0,))
                big = mm(qh, wv[i], d)
                res = big[:, :BS] + (big[:, BS:] + mm(ql, wv[i, :, :BS], d))
                for k in range(group):
                    ev[i % 2, g + k] = res[k * BS:(k + 1) * BS].T
            put_early(i).start()
            return carry

        lax.fori_loop(first, first + count, body, 0)

    def first_products(count):
        for t in range(n_near):
            for way in (0, 1, 3):
                halo(way, t).wait_recv()
        products(0, count)

    rounds = [k for k in range(len(stages)) if stages[k][3]]
    def begin():
        scatter(0)[0].start()

    def middle(k):
        scatter_end(k)
        scatter(k + 1)[0].start()

    def turn():
        scatter_end(len(stages) - 1)
        at = pl.ds(pl.multiple_of(offs[-1], 8), last)
        full[at] = acc[at]
        gather(rounds[-1]).start()

    def back(k, after):
        gather_end(k)
        gather(after).start()

    def finish():
        gather_end(rounds[0])
        scale()

    jobs = {}
    at_step = LAG
    for p in range(0, n_piece, 2):
        jobs[at_step] = functools.partial(gram, p, 2)
        at_step += 1
    jobs[at_step] = begin
    at_step += GAP
    for k in range(len(stages) - 1):
        jobs[at_step] = functools.partial(middle, k)
        at_step += GAP
    jobs[at_step] = turn
    at_step += GAP
    for k, after in zip(rounds[::-1][:-1], rounds[::-1][1:]):
        jobs[at_step] = functools.partial(back, k, after)
        at_step += GAP
    jobs[at_step] = finish
    for p in range(0, n_piece, 2):
        at_step += 1
        jobs[at_step] = functools.partial(adjoint, p, 2)
    at_step = max(at_step + 1, n_near + LAG + 1)
    quarter = n_blk // 4
    for p in range(0, n_blk, quarter):
        jobs[at_step] = (functools.partial(products, p, quarter) if p
                         else functools.partial(first_products, quarter))
        at_step += 2

    for t in range(max(n_chunk + LAG, max(jobs) + 1)):
        if t < n_chunk:
            if t >= WIN:
                for way in (0, 1, 2):
                    halo(way, t - WIN).wait_send()
            for way in (2, 0, 1):
                halo(way, t).start()
        if LAG <= t < n_chunk + LAG:
            if t >= LAG + WIN:
                halo(3, t - LAG - WIN).wait_send()
            halo(2, t - LAG).wait_recv()
            halo(3, t - LAG).start()
        if t in jobs:
            jobs[t]()

    put = pltpu.make_async_copy(wv, wcat, w_sem)
    put.start()
    for t in range(n_near, n_chunk):
        for way in (0, 1, 3):
            halo(way, t).wait_recv()
    for t in range(n_chunk - WIN, n_chunk):
        for way in (0, 1, 2, 3):
            halo(way, t).wait_send()
    put.wait()
    put_early(n_blk - 2).wait()
    put_early(n_blk - 1).wait()


def block_kernel(late, wcat, early, table, out, buf, sem):
    i = pl.program_id(0)
    n = pl.num_programs(0)
    n_nbr = buf.shape[1]
    d = ((1,), (0,))

    def fetch(step, k):
        slot = step % 2
        at = jnp.maximum(late[step, k], 0)
        return pltpu.make_async_copy(table.at[at], buf.at[slot, k], sem.at[slot, k])

    def fetch_all(step):
        for k in range(n_nbr):
            @pl.when(late[step, k] >= 0)
            def _():
                fetch(step, k).start()

    @pl.when(i == 0)
    def _():
        fetch_all(0)

    @pl.when(i + 1 < n)
    def _():
        fetch_all(i + 1)

    for k in range(n_nbr):
        @pl.when(late[i, k] >= 0)
        def _():
            fetch(i, k).wait()
            qh, ql = split(buf[i % 2, k])
            big = mm(qh, wcat[0], d)
            out[0, k] = (big[:, :BS] + (big[:, BS:] + mm(ql, wcat[0, :, :BS], d))).T

        @pl.when(late[i, k] < 0)
        def _():
            out[0, k] = early[0, k]


def body(n_row, n_sub, eig_vectors, vec_cotangent, levels, order, neighbours):
    rows, window = eig_vectors.shape
    n_blk = rows // BS
    n_nbr = neighbours.shape[1]
    n_chunk = rows // CHUNK
    eig = eig_vectors.reshape(n_chunk, CHUNK, window)
    cot = vec_cotangent.reshape(n_chunk, CHUNK, window)
    stages, last = stages_of(n_row, n_sub, window)
    n_rec = sum(s[2] // 2 if s[3] else s[2] for s in stages)
    any_spec = pl.BlockSpec(memory_space=pl.ANY)
    vmem_spec = pl.BlockSpec(memory_space=pltpu.VMEM)
    n_st = len(stages)
    near = n_blk * 5 // 8
    far = n_blk - near
    two = BS // CHUNK
    my_row = lax.axis_index("row")
    my_sub = lax.axis_index("sub")
    device = neighbours // n_blk
    local = neighbours % n_blk
    dev_row = device // n_sub
    dev_sub = device % n_sub
    pair_row = my_row + 1 - 2 * (my_row % 2)
    up = (my_sub + 1) % n_sub
    same_row = jnp.where(dev_sub == my_sub, -1, jnp.where(dev_sub == up, 1, 0))
    way = jnp.where(dev_row == my_row, same_row, jnp.where(dev_row == pair_row, 2, 3))
    is_late = (way >= 0) & (local >= near)
    picks = jnp.where(way < 0, local, jnp.where(is_late, 0, n_blk + way * near + local))
    late = jnp.where(is_late, way * far + local - near, -1)
    table, wcat, early = pl.pallas_call(
        functools.partial(halo_kernel, n_row, n_sub, stages, last),
        out_shape=[
            jax.ShapeDtypeStruct((4 * far * two, CHUNK, window), F32),
            jax.ShapeDtypeStruct((n_blk, window, 2 * BS), BF16),
            jax.ShapeDtypeStruct((n_blk, n_nbr, BS, BS), F32),
        ],
        in_specs=[any_spec, any_spec, vmem_spec, vmem_spec, pl.BlockSpec(memory_space=pltpu.SMEM)],
        out_specs=[any_spec, any_spec, any_spec],
        scratch_shapes=[
            pltpu.VMEM((n_chunk + 4 * near * two, CHUNK, window), F32),
            pltpu.VMEM((n_chunk, CHUNK, window), F32),
            pltpu.VMEM((2, n_nbr, BS, BS), F32),
            pltpu.VMEM((window, window), F32),
            pltpu.VMEM((window, window), F32),
            pltpu.VMEM((n_rec, window), F32),
            pltpu.VMEM((window, window), BF16),
            pltpu.VMEM((window, window), BF16),
            pltpu.VMEM((n_blk, window, 2 * BS), BF16),
            pltpu.SemaphoreType.DMA((2, rows // PIECE)),
            pltpu.SemaphoreType.DMA((2,)),
            pltpu.SemaphoreType.DMA,
            pltpu.SemaphoreType.DMA((4, n_chunk)),
            pltpu.SemaphoreType.DMA((4, n_chunk)),
            pltpu.SemaphoreType.DMA((2, n_st)),
            pltpu.SemaphoreType.DMA((2, n_st)),
        ],
        compiler_params=pltpu.CompilerParams(
            collective_id=0, has_side_effects=True, vmem_limit_bytes=48 * 2**20),
        name="halo",
    )(eig, cot, levels.reshape(1, window), order.reshape(1, window),
      picks.astype(jnp.int32))

    return pl.pallas_call(
        block_kernel,
        out_shape=jax.ShapeDtypeStruct((n_blk, n_nbr, BS, BS), F32),
        grid_spec=pltpu.PrefetchScalarGridSpec(
            num_scalar_prefetch=1,
            grid=(n_blk,),
            in_specs=[
                pl.BlockSpec((1, window, 2 * BS), lambda i, late: (i, 0, 0)),
                pl.BlockSpec((1, n_nbr, BS, BS), lambda i, late: (i, 0, 0, 0)),
                any_spec,
            ],
            out_specs=pl.BlockSpec((1, n_nbr, BS, BS), lambda i, late: (i, 0, 0, 0)),
            scratch_shapes=[
                pltpu.VMEM((2, n_nbr, BS, window), F32),
                pltpu.SemaphoreType.DMA((2, n_nbr)),
            ],
        ),
        compiler_params=pltpu.CompilerParams(vmem_limit_bytes=48 * 2**20),
        name="blocks",
    )(late.astype(jnp.int32), wcat, early, table.reshape(4 * far, BS, window))


def solution(mesh):
    in_specs = (P(("row", "sub"), None), P(("row", "sub"), None), P(), P(), P(("row", "sub"), None))
    out_specs = P(("row", "sub"), None, None, None)
    run = functools.partial(body, mesh.shape["row"], mesh.shape["sub"])
    return jax.shard_map(run, mesh=mesh, in_specs=in_specs, out_specs=out_specs, check_vma=False)
```
